32 devices in a mesh: grp: 2 (over x), rcv: 16 (over z, y, core).
Axes of the slice: x: 2, y: 2, z: 4, core: 2. Of those that a mesh axis runs over, the one named last changes fastest.
Arguments:
- reflection: bfloat16 [8, 2, 768, 768], P('grp', None, 'rcv'), parts along dimension 0, as said below
- direct_wave: float32 [32, 768, 256], P('grp', 'rcv'), parts along dimension 0, may hold values from -6 to 6
- mute_start_position: int32 [32, 768], P('grp', 'rcv'), parts along dimension 0, may hold values from 32 to 224
Outputs:
- downgoing: float32 [32, 768, 256], P('grp', 'rcv'), parts along dimension 0
- upgoing: float32 [32, 768, 256], P('grp', 'rcv'), parts along dimension 0
The draws below stay inside these ranges and needn't reach their ends.
There are 2 independent parts, one for each index of `grp`. The reference program is written for one: setup_inputs(seed, part) draws one part's arguments, and reference() takes and returns one part's arrays. A program takes and returns all parts, laid end to end along the dimension named above; each array names one. Nothing has to cross between parts.
Inputs may be any that keep to these rules, and one draw needn't show every extreme that they name: reflection is reciprocal: reflection[j, c, x, y] == reflection[j, c, y, x] for every bin j, part c and positions x, y.
All inputs are finite; a program needn't handle non-finite values.
Results may differ from the reference program's by a relative error of at most 0.006.
Values may be sent and summed in bfloat16 or wider, within the bound.
A program may use at most 64 MiB of HBM per device.

```python
import math
import jax
import jax.numpy as jnp
from jax import lax

FREQS = 4
FOCI = 16
RECORD_LENGTH = 256
ITERS = 4
N = 768


def draw_reflection(key, part):
    key = jax.random.fold_in(key, 7)
    slice_keys = jax.random.split(key, FREQS * 2)
    factor = (4.0 * N) ** (-0.5)

    def one_slice(slice_key):
        values = jax.random.normal(slice_key, (N, N), jnp.float32)
        return ((values + values.T) * factor).astype(jnp.bfloat16)
    return lax.map(one_slice, slice_keys).reshape(FREQS, 2, N, N)


def place_ends(entries, key, low, largest):
    longest = entries.shape.index(max(entries.shape))
    spots = []
    for shift in (0, 1):
        where = [jax.random.randint(jax.random.fold_in(key, axis), (), 0, length) for axis, length in enumerate(entries.shape)]
        where[longest] = (where[longest] + shift) % entries.shape[longest]
        spots.append(tuple(where))
    return entries.at[spots[0]].set(low).at[spots[1]].set(largest)


def shard_levels(rng, dims, pieces, least, top_value):
    gain, own = 1.0, jax.random.fold_in(rng, 6)
    for position, shards_of in pieces:
        heights = jnp.exp(jax.random.uniform(jax.random.fold_in(own, position), (shards_of,), jnp.float32, least / len(pieces), top_value / len(pieces)))
        gain = gain * jnp.repeat(heights, dims[position] // shards_of).reshape([-1 if axis == position else 1 for axis in range(len(dims))])
    return gain


def gaussian(key, dims, spread, limit, shards=(), kind=jnp.bfloat16):
    gain = shard_levels(key, dims, shards, -0.22, 0.18) if shards else 1.0
    values = jax.random.normal(key, dims, jnp.float32) * spread * gain
    return jnp.minimum(jnp.maximum(values, -limit), limit).astype(kind)


def setup_inputs(seed: int = 0, part: int = 0) -> dict:
    keys = jax.random.split(jax.random.key(seed), 4)
    own_keys = jax.random.split(jax.random.fold_in(keys[3], part), 4)
    reflection = draw_reflection(jax.random.fold_in(jax.random.fold_in(keys[3], part), 71), part)
    direct_wave = gaussian(own_keys[1], (FOCI, N, RECORD_LENGTH), 1.0, 6.0, ((1, 16),), jnp.float32)
    mute_start_position = place_ends(jax.random.randint(own_keys[2], (FOCI, N), RECORD_LENGTH // 8, 7 * RECORD_LENGTH // 8 + 1), jax.random.fold_in(own_keys[2], 1), RECORD_LENGTH // 8, (7 * RECORD_LENGTH // 8 + 1) - 1).astype(jnp.int32)
    return dict(reflection=reflection, direct_wave=direct_wave, mute_start_position=mute_start_position)


def fourier_tables():
    clock_moments = jnp.arange(RECORD_LENGTH, dtype=jnp.int32)
    temporal_pitches = (2 * jnp.arange(FREQS, dtype=jnp.int32) + 1) * (RECORD_LENGTH // (4 * FREQS))
    rotation_argument = clock_moments[:, None] * temporal_pitches[None, :] % RECORD_LENGTH
    angle = rotation_argument.astype(jnp.float32) * (2.0 * math.pi / RECORD_LENGTH)
    return (jnp.cos(angle), jnp.sin(angle))

def to_spectrum(wavefield, harmonic_real_grid, sine_table):
    factor = RECORD_LENGTH ** (-0.5)
    real_part = jnp.einsum('pxt,tf->xfp', wavefield, harmonic_real_grid, precision=lax.Precision.HIGHEST) * factor
    imag_part = -jnp.einsum('pxt,tf->xfp', wavefield, sine_table, precision=lax.Precision.HIGHEST) * factor
    return jnp.stack([real_part, imag_part], 2).astype(jnp.bfloat16)

def windowed(real_part, imag_part, mute_start_position, harmonic_real_grid, sine_table):
    factor = 3.0 / math.sqrt(RECORD_LENGTH)
    wavefield = jnp.einsum('xfp,tf->pxt', real_part, harmonic_real_grid, precision=lax.Precision.HIGHEST)
    wavefield = (wavefield - jnp.einsum('xfp,tf->pxt', imag_part, sine_table, precision=lax.Precision.HIGHEST)) * factor
    clock_moments = jnp.arange(RECORD_LENGTH, dtype=jnp.int32)
    mute_retained = clock_moments[None, None, :] < mute_start_position[:, :, None]
    return jnp.where(mute_retained, wavefield, jnp.zeros_like(wavefield))

def forward_conv(reflection, spectra):
    real_list, imag_list = ([], [])
    for freq in range(FREQS):
        operand = spectra[:, freq].reshape(N, 2 * FOCI)
        first = jnp.dot(reflection[freq, 0], operand, preferred_element_type=jnp.float32)
        second = jnp.dot(reflection[freq, 1], operand, preferred_element_type=jnp.float32)
        real_list.append(first[:, :FOCI] - second[:, FOCI:])
        imag_list.append(first[:, FOCI:] + second[:, :FOCI])
    return (jnp.stack(real_list, 1), jnp.stack(imag_list, 1))

def adjoint_conv(reflection, spectra):
    real_list, imag_list = ([], [])
    for freq in range(FREQS):
        operand = spectra[:, freq].reshape(N, 2 * FOCI)
        first = jnp.dot(operand.T, reflection[freq, 0], preferred_element_type=jnp.float32)
        second = jnp.dot(operand.T, reflection[freq, 1], preferred_element_type=jnp.float32)
        real_list.append((first[:FOCI] + second[FOCI:]).T)
        imag_list.append((first[FOCI:] - second[:FOCI]).T)
    return (jnp.stack(real_list, 1), jnp.stack(imag_list, 1))

def reference(reflection, direct_wave, mute_start_position):
    harmonic_real_grid, sine_table = fourier_tables()
    downgoing = direct_wave
    upgoing = direct_wave
    for iteration in range(ITERS):
        spectra = to_spectrum(downgoing, harmonic_real_grid, sine_table)
        real_part, imag_part = forward_conv(reflection, spectra)
        upgoing = windowed(real_part, imag_part, mute_start_position, harmonic_real_grid, sine_table)
        back_spectra = to_spectrum(upgoing, harmonic_real_grid, sine_table)
        back_real, back_imag = adjoint_conv(reflection, back_spectra)
        downgoing = direct_wave + windowed(back_real, back_imag, mute_start_position, harmonic_real_grid, sine_table)
    return (downgoing, upgoing)
```

```python
import functools
import math

import jax
import jax.numpy as jnp
from jax import lax
from jax.experimental import pallas as pl
from jax.experimental.pallas import tpu as pltpu
from jax.sharding import PartitionSpec as P

ITERS = 4
LANES = 128
NT = (((1,), (1,)), ((), ()))
TN = (((0,), (0,)), ((), ()))
MESH = pl.DeviceIdType.MESH


def tables(freqs):
    phases = 2 * freqs
    period = 2 * phases
    angle = [
        [2.0 * math.pi * ((r * (2 * j + 1)) % period) / period for j in range(freqs)]
        for r in range(phases)
    ]
    cosine = [[math.cos(a) for a in row] for row in angle]
    sine = [[math.sin(a) for a in row] for row in angle]
    return cosine, sine


def combs(rows, phases, ticks):
    row = lax.broadcasted_iota(jnp.int32, (rows, ticks), 0) % phases
    tick = lax.broadcasted_iota(jnp.int32, (rows, ticks), 1)
    sign = (1 - 2 * ((tick // phases) % 2)).astype(jnp.float32)
    return jnp.where(tick % phases == row, sign, 0.0).astype(jnp.bfloat16)


def add_up(terms):
    terms = list(terms)
    while len(terms) > 1:
        pairs = [a + b for a, b in zip(terms[::2], terms[1::2])]
        terms = pairs + ([terms[-1]] if len(terms) % 2 else [])
    return terms[0]


def iterate(
    devices, freqs, foci, rows, ticks,
    refl_ref, direct_ref, mute_ref, out_ref,
    matrix, spectra, own, other, kept, leave, arrive,
    matrix_send, matrix_recv, own_send, own_recv,
    block_send, block_recv, last_send, last_recv,
):
    chips = devices // 2
    pairs = chips // 2
    phases = 2 * freqs
    half = foci // 2
    width = 2 * rows
    deep = 2 * half
    me = lax.axis_index("rcv")
    core = me % 2
    chip = me // 2
    twin = chip * 2 + (1 - core)
    cosine, sine = tables(freqs)

    barrier = pltpu.get_barrier_semaphore()
    pl.semaphore_signal(barrier, inc=1, device_id={"rcv": twin}, device_id_type=MESH)

    def greet(d, carry):
        there = ((chip + d) % chips) * 2 + core
        pl.semaphore_signal(barrier, inc=1, device_id={"rcv": there}, device_id_type=MESH)
        return carry

    lax.fori_loop(1, chips, greet, 0)

    own[...] = jnp.zeros_like(own)
    comb = combs(2 * phases, phases, ticks)
    for p in range(foci):
        wave = direct_ref[p]
        high = wave.astype(jnp.bfloat16)
        low = (wave - high.astype(jnp.float32)).astype(jnp.bfloat16)
        sums = lax.dot_general(comb, high, NT, preferred_element_type=jnp.float32)
        sums += lax.dot_general(comb, low, NT, preferred_element_type=jnp.float32)
        own[0:phases, p, 0:rows] = sums[0:phases]
    own[phases, :, 0:rows] = mute_ref[...].astype(jnp.float32)

    pl.semaphore_wait(barrier, chips)

    own_copy = pltpu.make_async_remote_copy(
        src_ref=own.at[:, pl.ds(pl.multiple_of((1 - core) * half, 8), half), :],
        dst_ref=other,
        send_sem=own_send,
        recv_sem=own_recv,
        device_id={"rcv": twin},
        device_id_type=MESH,
    )
    own_copy.start()

    place = pl.ds(pl.multiple_of(core * rows, 16), rows)
    rest = LANES - width
    for j in range(freqs):
        for c in range(2):
            if rest:
                matrix[:, j, c, width:LANES, :] = jnp.zeros((pairs, rest, 2 * LANES), jnp.bfloat16)
            for k in range(chips):
                part = refl_ref[j, c, :, k * width : (k + 1) * width]
                if rest:
                    part = jnp.concatenate([part, jnp.zeros((rows, rest), jnp.bfloat16)], 1)
                matrix[k // 2, j, c, place, (k % 2) * LANES : (k % 2 + 1) * LANES] = part
    matrix_copy = pltpu.make_async_remote_copy(
        src_ref=matrix.at[:, :, :, place, :],
        dst_ref=matrix.at[:, :, :, place, :],
        send_sem=matrix_send,
        recv_sem=matrix_recv,
        device_id={"rcv": twin},
        device_id_type=MESH,
    )
    matrix_copy.start()

    own_copy.wait()

    def whole(a, b):
        left = jnp.where(core == 0, a, b)
        right = jnp.where(core == 0, b, a)
        return left + pltpu.roll(right, rows, 1)

    mine = pl.ds(pl.multiple_of(core * half, 8), half)
    sums = [whole(own[r, mine, :], other[r]) for r in range(phases + 1)]
    ends = sums.pop()
    counts = [jnp.floor((ends + (phases - 1 - r)) * (1.0 / phases)) for r in range(phases)]

    def to_spectrum(values, scale):
        lines = []
        for j in range(freqs):
            lines.append(add_up(values[r] * (scale * cosine[r][j]) for r in range(phases)))
            lines.append(add_up(values[r] * (-scale * sine[r][j]) for r in range(phases)))
        return lines

    def to_phases(lines, scale):
        return [
            add_up(
                lines[2 * j + c] * (scale * (cosine[r][j], -sine[r][j])[c])
                for j in range(freqs)
                for c in range(2)
            )
            for r in range(phases)
        ]

    first = to_spectrum(sums, ticks**-0.5)

    def block_copy(slot, d):
        there = ((chip + d) % chips) * 2 + core
        ours = spectra.at[slot, chip]
        return pltpu.make_async_remote_copy(
            src_ref=ours,
            dst_ref=ours,
            send_sem=block_send.at[slot, d],
            recv_sem=block_recv.at[slot, chip],
            device_id={"rcv": there},
            device_id_type=MESH,
        )

    def arrival(slot, source):
        theirs = spectra.at[slot, source]
        return pltpu.make_async_remote_copy(
            src_ref=theirs,
            dst_ref=theirs,
            send_sem=block_send.at[slot, 0],
            recv_sem=block_recv.at[slot, source],
            device_id={"rcv": me},
            device_id_type=MESH,
        )

    pair = chip // 2

    def convolve(slot, lines, sign):
        block = jnp.concatenate(lines, 0).astype(jnp.bfloat16)
        spectra[slot, chip] = block

        def send(d, carry):
            block_copy(slot, d).start()
            return carry

        lax.fori_loop(1, chips, send, 0, unroll=chips <= 8)
        arrival(slot, chip + 1 - 2 * (chip % 2)).wait_recv()

        def multiply(at, totals):
            out = []
            for j in range(freqs):
                left = jnp.concatenate(
                    [spectra[slot, 2 * at + h, deep * j : deep * (j + 1), :] for h in range(2)], 1
                )
                right = matrix[at, j].reshape(2 * LANES, 2 * LANES)
                out.append(
                    totals[j]
                    + lax.dot_general(left, right, NT, preferred_element_type=jnp.float32)
                )
            return tuple(out)

        totals = tuple(jnp.zeros((deep, 2 * LANES), jnp.float32) for _ in range(freqs))
        totals = multiply(pair, totals)

        def step(d, totals):
            at = (pair + d) % pairs
            arrival(slot, 2 * at).wait_recv()
            arrival(slot, 2 * at + 1).wait_recv()
            return multiply(at, totals)

        totals = lax.fori_loop(1, pairs, step, totals, unroll=chips <= 8)

        def sent(d, carry):
            block_copy(slot, d).wait_send()
            return carry

        lax.fori_loop(1, chips, sent, 0, unroll=chips <= 8)
        result = []
        for t in totals:
            result.append(t[0:half, 0:LANES] - sign * t[half:deep, LANES:])
            result.append(t[half:deep, 0:LANES] + sign * t[0:half, LANES:])
        return result

    matrix_copy.wait()

    def iteration(_, lines):
        up = to_phases(convolve(0, lines, 1.0), 3.0 * ticks**-0.5)
        for r in range(phases):
            kept[0, r] = up[r]
        back = to_spectrum([u * n for u, n in zip(up, counts)], ticks**-0.5)
        down = to_phases(convolve(1, back, -1.0), 3.0 * ticks**-0.5)
        for r in range(phases):
            kept[1, r] = down[r]
        change = to_spectrum([u * n for u, n in zip(down, counts)], ticks**-0.5)
        return tuple(a + b for a, b in zip(first, change))

    lax.fori_loop(0, ITERS, iteration, tuple(first))

    for u in range(2):
        for r in range(phases):
            wave = kept[u, r]
            turned = pltpu.roll(wave, LANES - rows, 1)
            out_ref[pl.ds(core * half, half), u, r, :] = jnp.where(core == 0, wave, turned)
            leave[u, r] = jnp.where(core == 0, turned, wave)
    last_copy = pltpu.make_async_remote_copy(
        src_ref=leave,
        dst_ref=arrive,
        send_sem=last_send,
        recv_sem=last_recv,
        device_id={"rcv": twin},
        device_id_type=MESH,
    )
    last_copy.start()
    last_copy.wait()
    for u in range(2):
        for r in range(phases):
            out_ref[pl.ds((1 - core) * half, half), u, r, :] = arrive[u, r]


def spread(phases, rows, ticks, count, waves_ref, direct_ref, mute_ref, down_ref, up_ref):
    foci = mute_ref.shape[0]
    base = pl.program_id(0) * count
    comb = combs(4 * phases, phases, ticks)
    ends = mute_ref[...].astype(jnp.float32).astype(jnp.bfloat16)
    lane = lax.broadcasted_iota(jnp.int32, (rows, ticks), 1).astype(jnp.float32)
    which = lax.broadcasted_iota(jnp.int32, (foci, ticks), 0)
    for i in range(count):
        pick = jnp.where(which == base + i, 1.0, 0.0).astype(jnp.bfloat16)
        end = lax.dot_general(ends, pick, TN, preferred_element_type=jnp.float32)
        inside = lane < end
        for u, ref in ((0, up_ref), (1, down_ref)):
            wave = waves_ref[i, u]
            high = wave.astype(jnp.bfloat16).astype(jnp.float32)
            mid = (wave - high).astype(jnp.bfloat16).astype(jnp.float32)
            low = wave - high - mid
            parts = jnp.concatenate([high, mid, low, jnp.zeros_like(low)], 0).astype(jnp.bfloat16)
            field = lax.dot_general(parts, comb, TN, preferred_element_type=jnp.float32)[0:rows]
            field = jnp.where(inside, field, 0.0)
            ref[i] = field if u == 0 else direct_ref[i] + field


def per_device(devices, reflection, direct_wave, mute_start_position):
    freqs = reflection.shape[0]
    foci, rows, ticks = direct_wave.shape
    chips = devices // 2
    phases = 2 * freqs
    half = foci // 2
    vmem = pl.BlockSpec(memory_space=pltpu.VMEM)
    dma = pltpu.SemaphoreType.DMA
    waves = pl.pallas_call(
        functools.partial(iterate, devices, freqs, foci, rows, ticks),
        out_shape=jax.ShapeDtypeStruct((foci, 2, phases, LANES), jnp.float32),
        in_specs=[vmem] * 3,
        out_specs=vmem,
        scratch_shapes=[
            pltpu.VMEM((chips // 2, freqs, 2, LANES, 2 * LANES), jnp.bfloat16),
            pltpu.VMEM((2, chips, 2 * freqs * half, LANES), jnp.bfloat16),
            pltpu.VMEM((phases + 1, foci, LANES), jnp.float32),
            pltpu.VMEM((phases + 1, half, LANES), jnp.float32),
            pltpu.VMEM((2, phases, half, LANES), jnp.float32),
            pltpu.VMEM((2, phases, half, LANES), jnp.float32),
            pltpu.VMEM((2, phases, half, LANES), jnp.float32),
            dma, dma, dma, dma,
            dma((2, chips)), dma((2, chips)),
            dma, dma,
        ],
        compiler_params=pltpu.CompilerParams(
            collective_id=0, has_side_effects=True, vmem_limit_bytes=48 * 2**20
        ),
    )(reflection, direct_wave, mute_start_position)
    count = 4
    return tuple(
        pl.pallas_call(
            functools.partial(spread, phases, rows, ticks, count),
            grid=(foci // count,),
            out_shape=[jax.ShapeDtypeStruct(direct_wave.shape, jnp.float32)] * 2,
            in_specs=[
                pl.BlockSpec((count, 2, phases, LANES), lambda i: (i, 0, 0, 0)),
                pl.BlockSpec((count, rows, ticks), lambda i: (i, 0, 0)),
                pl.BlockSpec((foci, rows), lambda i: (0, 0)),
            ],
            out_specs=[pl.BlockSpec((count, rows, ticks), lambda i: (i, 0, 0))] * 2,
            compiler_params=pltpu.CompilerParams(vmem_limit_bytes=16 * 2**20),
        )(waves, direct_wave, mute_start_position)
    )


def solution(mesh):
    placed = (P("grp", None, "rcv", None), P("grp", "rcv", None), P("grp", "rcv"))
    return jax.shard_map(
        functools.partial(per_device, mesh.shape["rcv"]),
        mesh=mesh,
        in_specs=placed,
        out_specs=(P("grp", "rcv", None), P("grp", "rcv", None)),
        check_vma=False,
    )
```

```python
import functools
import math

import jax
import jax.numpy as jnp
from jax import lax
from jax.experimental import pallas as pl
from jax.experimental.pallas import tpu as pltpu
from jax.sharding import PartitionSpec as P

ITERS = 4
LANES = 128
NT = (((1,), (1,)), ((), ()))
TN = (((0,), (0,)), ((), ()))
MESH = pl.DeviceIdType.MESH


def tables(freqs):
    phases = 2 * freqs
    period = 2 * phases
    angle = [
        [2.0 * math.pi * ((r * (2 * j + 1)) % period) / period for j in range(freqs)]
        for r in range(phases)
    ]
    cosine = [[math.cos(a) for a in row] for row in angle]
    sine = [[math.sin(a) for a in row] for row in angle]
    return cosine, sine


def combs(rows, phases, ticks):
    row = lax.broadcasted_iota(jnp.int32, (rows, ticks), 0) % phases
    tick = lax.broadcasted_iota(jnp.int32, (rows, ticks), 1)
    sign = (1 - 2 * ((tick // phases) % 2)).astype(jnp.float32)
    return jnp.where(tick % phases == row, sign, 0.0).astype(jnp.bfloat16)


def add_up(terms):
    terms = list(terms)
    while len(terms) > 1:
        pairs = [a + b for a, b in zip(terms[::2], terms[1::2])]
        terms = pairs + ([terms[-1]] if len(terms) % 2 else [])
    return terms[0]


def iterate(
    devices, freqs, foci, rows, ticks,
    refl_hbm, direct_hbm, mute_hbm, out_ref,
    refl_ref, direct_ref, mute_ref, matrix, spectra, own, other, leave, arrive,
    fetched, matrix_send, matrix_recv, own_send, own_recv,
    block_send, block_recv, last_send, last_recv,
):
    chips = devices // 2
    pairs = chips // 2
    phases = 2 * freqs
    half = foci // 2
    width = 2 * rows
    deep = 2 * half
    me = lax.axis_index("rcv")
    core = me % 2
    chip = me // 2
    twin = chip * 2 + (1 - core)
    cosine, sine = tables(freqs)

    theirs_half = pl.ds((1 - core) * half, half)
    ours_half = pl.ds(core * half, half)
    fetches = [
        pltpu.make_async_copy(direct_hbm.at[theirs_half], direct_ref.at[theirs_half], fetched.at[0]),
        pltpu.make_async_copy(mute_hbm, mute_ref, fetched.at[1]),
        pltpu.make_async_copy(direct_hbm.at[ours_half], direct_ref.at[ours_half], fetched.at[2]),
        pltpu.make_async_copy(refl_hbm, refl_ref, fetched.at[3]),
    ]
    for fetch in fetches:
        fetch.start()

    barrier = pltpu.get_barrier_semaphore()
    pl.semaphore_signal(barrier, inc=1, device_id={"rcv": twin}, device_id_type=MESH)

    def greet(d, carry):
        there = ((chip + d) % chips) * 2 + core
        pl.semaphore_signal(barrier, inc=1, device_id={"rcv": there}, device_id_type=MESH)
        return carry

    lax.fori_loop(1, chips, greet, 0)

    own[...] = jnp.zeros_like(own)
    comb = combs(2 * phases, phases, ticks)

    def sum_phases(start):
        for i in range(half):
            p = start + i
            wave = direct_ref[p]
            high = wave.astype(jnp.bfloat16)
            low = (wave - high.astype(jnp.float32)).astype(jnp.bfloat16)
            sums = lax.dot_general(comb, high, NT, preferred_element_type=jnp.float32)
            sums += lax.dot_general(comb, low, NT, preferred_element_type=jnp.float32)
            own[0:phases, p, 0:rows] = sums[0:phases]

    fetches[0].wait()
    sum_phases((1 - core) * half)
    fetches[1].wait()
    own[phases, :, 0:rows] = mute_ref[...].astype(jnp.float32)

    pl.semaphore_wait(barrier, chips)

    own_copy = pltpu.make_async_remote_copy(
        src_ref=own.at[:, pl.ds(pl.multiple_of((1 - core) * half, 8), half), :],
        dst_ref=other,
        send_sem=own_send,
        recv_sem=own_recv,
        device_id={"rcv": twin},
        device_id_type=MESH,
    )
    own_copy.start()
    fetches[2].wait()
    sum_phases(core * half)
    fetches[3].wait()

    place = pl.ds(pl.multiple_of(core * rows, 16), rows)
    rest = LANES - width
    for j in range(freqs):
        for c in range(2):
            if rest:
                matrix[:, j, c, width:LANES, :] = jnp.zeros((pairs, rest, 2 * LANES), jnp.bfloat16)
            for k in range(chips):
                part = refl_ref[j, c, :, k * width : (k + 1) * width]
                if rest:
                    part = jnp.concatenate([part, jnp.zeros((rows, rest), jnp.bfloat16)], 1)
                matrix[k // 2, j, c, place, (k % 2) * LANES : (k % 2 + 1) * LANES] = part
    matrix_copy = pltpu.make_async_remote_copy(
        src_ref=matrix.at[:, :, :, place, :],
        dst_ref=matrix.at[:, :, :, place, :],
        send_sem=matrix_send,
        recv_sem=matrix_recv,
        device_id={"rcv": twin},
        device_id_type=MESH,
    )
    matrix_copy.start()

    own_copy.wait()

    def whole(a, b):
        left = jnp.where(core == 0, a, b)
        right = jnp.where(core == 0, b, a)
        return left + pltpu.roll(right, rows, 1)

    mine = pl.ds(pl.multiple_of(core * half, 8), half)
    sums = [whole(own[r, mine, :], other[r]) for r in range(phases + 1)]
    ends = sums.pop()
    counts = [jnp.floor((ends + (phases - 1 - r)) * (1.0 / phases)) for r in range(phases)]

    def to_spectrum(values, scale):
        lines = []
        for j in range(freqs):
            lines.append(add_up(values[r] * (scale * cosine[r][j]) for r in range(phases)))
            lines.append(add_up(values[r] * (-scale * sine[r][j]) for r in range(phases)))
        return lines

    def to_phases(lines, scale):
        return [
            add_up(
                lines[2 * j + c] * (scale * (cosine[r][j], -sine[r][j])[c])
                for j in range(freqs)
                for c in range(2)
            )
            for r in range(phases)
        ]

    first = to_spectrum(sums, ticks**-0.5)

    small = chips == 8

    def partner(number, d):
        if not small:
            return (number + d) % chips
        flipped = 0
        for bit in (4, 2, 1):
            now = (number // bit) % 2
            flipped += bit * (1 - now if d & bit else now)
        return flipped

    def each_partner(body):
        if small:
            for d in range(chips - 1, 0, -1):
                body(d, 0)
        else:
            lax.fori_loop(1, chips, body, 0)

    def block_copy(slot, d):
        there = partner(chip, d) * 2 + core
        ours = spectra.at[slot, chip]
        return pltpu.make_async_remote_copy(
            src_ref=ours,
            dst_ref=ours,
            send_sem=block_send.at[slot, d],
            recv_sem=block_recv.at[slot, chip],
            device_id={"rcv": there},
            device_id_type=MESH,
        )

    def arrival(slot, source):
        theirs = spectra.at[slot, source]
        return pltpu.make_async_remote_copy(
            src_ref=theirs,
            dst_ref=theirs,
            send_sem=block_send.at[slot, 0],
            recv_sem=block_recv.at[slot, source],
            device_id={"rcv": me},
            device_id_type=MESH,
        )

    pair = chip // 2

    def convolve(slot, lines, sign, meanwhile=None):
        block = jnp.concatenate(lines, 0).astype(jnp.bfloat16)
        spectra[slot, chip] = block

        def send(d, carry):
            block_copy(slot, d).start()
            return carry

        each_partner(send)
        if meanwhile is not None:
            meanwhile()
        arrival(slot, chip + 1 - 2 * (chip % 2)).wait_recv()

        def multiply(at, totals):
            out = []
            for j in range(freqs):
                left = jnp.concatenate(
                    [spectra[slot, 2 * at + h, deep * j : deep * (j + 1), :] for h in range(2)], 1
                )
                right = matrix[at, j].reshape(2 * LANES, 2 * LANES)
                out.append(
                    totals[j]
                    + lax.dot_general(left, right, NT, preferred_element_type=jnp.float32)
                )
            return tuple(out)

        totals = tuple(jnp.zeros((deep, 2 * LANES), jnp.float32) for _ in range(freqs))
        totals = multiply(pair, totals)

        def step(d, totals):
            at = partner(chip, 2 * d) // 2 if small else (pair + d) % pairs
            arrival(slot, 2 * at).wait_recv()
            arrival(slot, 2 * at + 1).wait_recv()
            return multiply(at, totals)

        if small:
            for d in range(1, pairs):
                totals = step(d, totals)
        else:
            totals = lax.fori_loop(1, pairs, step, totals)

        def sent(d, carry):
            block_copy(slot, d).wait_send()
            return carry

        each_partner(sent)
        result = []
        for t in totals:
            result.append(t[0:half, 0:LANES] - sign * t[half:deep, LANES:])
            result.append(t[half:deep, 0:LANES] + sign * t[0:half, LANES:])
        return result

    def last_copy(u):
        return pltpu.make_async_remote_copy(
            src_ref=leave.at[u],
            dst_ref=arrive.at[u],
            send_sem=last_send.at[u],
            recv_sem=last_recv.at[u],
            device_id={"rcv": twin},
            device_id_type=MESH,
        )

    def hand_over(u, waves):
        turned = [pltpu.roll(wave, LANES - rows, 1) for wave in waves]
        for r in range(phases):
            leave[u, r] = jnp.where(core == 0, turned[r], waves[r])
        last_copy(u).start()
        for r in range(phases):
            out_ref[ours_half, u, r, :] = jnp.where(core == 0, waves[r], turned[r])

    def take_over(u):
        last_copy(u).wait()
        for r in range(phases):
            out_ref[theirs_half, u, r, :] = arrive[u, r]

    lines = first
    for iteration in range(ITERS):
        last = iteration == ITERS - 1
        forward = convolve(0, lines, 1.0, None if iteration else matrix_copy.wait)
        up = to_phases(forward, 3.0 * ticks**-0.5)
        back = to_spectrum([u * n for u, n in zip(up, counts)], ticks**-0.5)
        adjoint = convolve(1, back, -1.0, functools.partial(hand_over, 0, up) if last else None)
        down = to_phases(adjoint, 3.0 * ticks**-0.5)
        if not last:
            change = to_spectrum([u * n for u, n in zip(down, counts)], ticks**-0.5)
            lines = [a + b for a, b in zip(first, change)]
    hand_over(1, down)
    take_over(0)
    take_over(1)


def spread(phases, rows, ticks, count, waves_ref, direct_ref, mute_ref, down_ref, up_ref):
    foci = mute_ref.shape[0]
    base = pl.program_id(0) * count
    comb = combs(4 * phases, phases, ticks)
    ends = mute_ref[...].astype(jnp.float32).astype(jnp.bfloat16)
    lane = lax.broadcasted_iota(jnp.int32, (rows, ticks), 1).astype(jnp.float32)
    which = lax.broadcasted_iota(jnp.int32, (foci, ticks), 0)
    for i in range(count):
        pick = jnp.where(which == base + i, 1.0, 0.0).astype(jnp.bfloat16)
        end = lax.dot_general(ends, pick, TN, preferred_element_type=jnp.float32)
        inside = lane < end
        for u, ref in ((0, up_ref), (1, down_ref)):
            wave = waves_ref[i, u]
            high = wave.astype(jnp.bfloat16).astype(jnp.float32)
            mid = (wave - high).astype(jnp.bfloat16).astype(jnp.float32)
            low = wave - high - mid
            parts = jnp.concatenate([high, mid, low, jnp.zeros_like(low)], 0).astype(jnp.bfloat16)
            field = lax.dot_general(parts, comb, TN, preferred_element_type=jnp.float32)[0:rows]
            field = jnp.where(inside, field, 0.0)
            ref[i] = field if u == 0 else direct_ref[i] + field


def per_device(devices, reflection, direct_wave, mute_start_position):
    freqs = reflection.shape[0]
    foci, rows, ticks = direct_wave.shape
    chips = devices // 2
    phases = 2 * freqs
    half = foci // 2
    vmem = pl.BlockSpec(memory_space=pltpu.VMEM)
    dma = pltpu.SemaphoreType.DMA
    waves = pl.pallas_call(
        functools.partial(iterate, devices, freqs, foci, rows, ticks),
        out_shape=jax.ShapeDtypeStruct((foci, 2, phases, LANES), jnp.float32),
        in_specs=[pl.BlockSpec(memory_space=pl.ANY)] * 3,
        out_specs=vmem,
        scratch_shapes=[
            pltpu.VMEM(reflection.shape, jnp.bfloat16),
            pltpu.VMEM(direct_wave.shape, jnp.float32),
            pltpu.VMEM(mute_start_position.shape, jnp.int32),
            pltpu.VMEM((chips // 2, freqs, 2, LANES, 2 * LANES), jnp.bfloat16),
            pltpu.VMEM((2, chips, 2 * freqs * half, LANES), jnp.bfloat16),
            pltpu.VMEM((phases + 1, foci, LANES), jnp.float32),
            pltpu.VMEM((phases + 1, half, LANES), jnp.float32),
            pltpu.VMEM((2, phases, half, LANES), jnp.float32),
            pltpu.VMEM((2, phases, half, LANES), jnp.float32),
            dma((4,)), dma, dma, dma, dma,
            dma((2, chips)), dma((2, chips)),
            dma((2,)), dma((2,)),
        ],
        compiler_params=pltpu.CompilerParams(
            collective_id=0, has_side_effects=True, vmem_limit_bytes=48 * 2**20
        ),
    )(reflection, direct_wave, mute_start_position)
    count = 4
    return tuple(
        pl.pallas_call(
            functools.partial(spread, phases, rows, ticks, count),
            grid=(foci // count,),
            out_shape=[jax.ShapeDtypeStruct(direct_wave.shape, jnp.float32)] * 2,
            in_specs=[
                pl.BlockSpec((count, 2, phases, LANES), lambda i: (i, 0, 0, 0)),
                pl.BlockSpec((count, rows, ticks), lambda i: (i, 0, 0)),
                pl.BlockSpec((foci, rows), lambda i: (0, 0)),
            ],
            out_specs=[pl.BlockSpec((count, rows, ticks), lambda i: (i, 0, 0))] * 2,
            compiler_params=pltpu.CompilerParams(vmem_limit_bytes=16 * 2**20),
        )(waves, direct_wave, mute_start_position)
    )


def solution(mesh):
    placed = (P("grp", None, "rcv", None), P("grp", "rcv", None), P("grp", "rcv"))
    return jax.shard_map(
        functools.partial(per_device, mesh.shape["rcv"]),
        mesh=mesh,
        in_specs=placed,
        out_specs=(P("grp", "rcv", None), P("grp", "rcv", None)),
        check_vma=False,
    )
```

```python
import functools
import math

import jax
import jax.numpy as jnp
from jax import lax
from jax.experimental import pallas as pl
from jax.experimental.pallas import tpu as pltpu
from jax.sharding import PartitionSpec as P

ITERS = 4
LANES = 128
NT = (((1,), (1,)), ((), ()))
TN = (((0,), (0,)), ((), ()))
MESH = pl.DeviceIdType.MESH


def tables(freqs):
    phases = 2 * freqs
    period = 2 * phases
    angle = [
        [2.0 * math.pi * ((r * (2 * j + 1)) % period) / period for j in range(freqs)]
        for r in range(phases)
    ]
    cosine = [[math.cos(a) for a in row] for row in angle]
    sine = [[math.sin(a) for a in row] for row in angle]
    return cosine, sine


def combs(rows, phases, ticks):
    row = lax.broadcasted_iota(jnp.int32, (rows, ticks), 0) % phases
    tick = lax.broadcasted_iota(jnp.int32, (rows, ticks), 1)
    sign = (1 - 2 * ((tick // phases) % 2)).astype(jnp.float32)
    return jnp.where(tick % phases == row, sign, 0.0).astype(jnp.bfloat16)


def add_up(terms):
    terms = list(terms)
    while len(terms) > 1:
        pairs = [a + b for a, b in zip(terms[::2], terms[1::2])]
        terms = pairs + ([terms[-1]] if len(terms) % 2 else [])
    return terms[0]


def iterate(
    devices, freqs, foci, rows, ticks,
    refl_hbm, direct_hbm, mute_hbm, out_ref,
    refl_ref, direct_ref, mute_ref, matrix, spectra, own, other, leave, arrive,
    fetched, matrix_send, matrix_recv, own_send, own_recv,
    block_send, block_recv, last_send, last_recv,
):
    chips = devices // 2
    pairs = chips // 2
    phases = 2 * freqs
    half = foci // 2
    width = 2 * rows
    deep = 2 * half
    me = lax.axis_index("rcv")
    core = me % 2
    chip = me // 2
    twin = chip * 2 + (1 - core)
    cosine, sine = tables(freqs)

    theirs_half = pl.ds((1 - core) * half, half)
    ours_half = pl.ds(core * half, half)
    fetches = [
        pltpu.make_async_copy(direct_hbm.at[theirs_half], direct_ref.at[theirs_half], fetched.at[0]),
        pltpu.make_async_copy(mute_hbm, mute_ref, fetched.at[1]),
        pltpu.make_async_copy(direct_hbm.at[ours_half], direct_ref.at[ours_half], fetched.at[2]),
        pltpu.make_async_copy(refl_hbm, refl_ref, fetched.at[3]),
    ]
    for fetch in fetches:
        fetch.start()

    barrier = pltpu.get_barrier_semaphore()
    pl.semaphore_signal(barrier, inc=1, device_id={"rcv": twin}, device_id_type=MESH)

    def greet(d, carry):
        there = ((chip + d) % chips) * 2 + core
        pl.semaphore_signal(barrier, inc=1, device_id={"rcv": there}, device_id_type=MESH)
        return carry

    lax.fori_loop(1, chips, greet, 0)

    own[...] = jnp.zeros_like(own)
    comb = combs(2 * phases, phases, ticks)

    def sum_phases(start):
        for i in range(half):
            p = start + i
            wave = direct_ref[p]
            high = wave.astype(jnp.bfloat16)
            low = (wave - high.astype(jnp.float32)).astype(jnp.bfloat16)
            sums = lax.dot_general(comb, high, NT, preferred_element_type=jnp.float32)
            sums += lax.dot_general(comb, low, NT, preferred_element_type=jnp.float32)
            own[0:phases, p, 0:rows] = sums[0:phases]

    fetches[0].wait()
    sum_phases((1 - core) * half)
    fetches[1].wait()
    own[phases, :, 0:rows] = mute_ref[...].astype(jnp.float32)

    pl.semaphore_wait(barrier, chips)

    own_copy = pltpu.make_async_remote_copy(
        src_ref=own.at[:, pl.ds(pl.multiple_of((1 - core) * half, 8), half), :],
        dst_ref=other,
        send_sem=own_send,
        recv_sem=own_recv,
        device_id={"rcv": twin},
        device_id_type=MESH,
    )
    own_copy.start()
    fetches[2].wait()
    sum_phases(core * half)
    fetches[3].wait()

    place = pl.ds(pl.multiple_of(core * rows, 16), rows)
    rest = LANES - width
    for j in range(freqs):
        for c in range(2):
            if rest:
                matrix[:, j, c, width:LANES, :] = jnp.zeros((pairs, rest, 2 * LANES), jnp.bfloat16)
            for k in range(chips):
                part = refl_ref[j, c, :, k * width : (k + 1) * width]
                if rest:
                    part = jnp.concatenate([part, jnp.zeros((rows, rest), jnp.bfloat16)], 1)
                matrix[k // 2, j, c, place, (k % 2) * LANES : (k % 2 + 1) * LANES] = part
    matrix_copy = pltpu.make_async_remote_copy(
        src_ref=matrix.at[:, :, :, place, :],
        dst_ref=matrix.at[:, :, :, place, :],
        send_sem=matrix_send,
        recv_sem=matrix_recv,
        device_id={"rcv": twin},
        device_id_type=MESH,
    )
    matrix_copy.start()

    own_copy.wait()

    def whole(a, b):
        left = jnp.where(core == 0, a, b)
        right = jnp.where(core == 0, b, a)
        return left + pltpu.roll(right, rows, 1)

    mine = pl.ds(pl.multiple_of(core * half, 8), half)
    sums = [whole(own[r, mine, :], other[r]) for r in range(phases + 1)]
    ends = sums.pop()
    counts = [jnp.floor((ends + (phases - 1 - r)) * (1.0 / phases)) for r in range(phases)]

    def to_spectrum(values, scale):
        lines = []
        for j in range(freqs):
            lines.append(add_up(values[r] * (scale * cosine[r][j]) for r in range(phases)))
            lines.append(add_up(values[r] * (-scale * sine[r][j]) for r in range(phases)))
        return lines

    def to_phases(lines, scale):
        return [
            add_up(
                lines[2 * j + c] * (scale * (cosine[r][j], -sine[r][j])[c])
                for j in range(freqs)
                for c in range(2)
            )
            for r in range(phases)
        ]

    first = to_spectrum(sums, ticks**-0.5)

    small = chips == 8

    def partner(number, d):
        if not small:
            return (number + d) % chips
        flipped = 0
        for bit in (4, 2, 1):
            now = (number // bit) % 2
            flipped += bit * (1 - now if d & bit else now)
        return flipped

    def each_partner(body):
        if small:
            for d in range(chips - 1, 0, -1):
                body(d, 0)
        else:
            lax.fori_loop(1, chips, body, 0)

    def block_copy(slot, d):
        there = partner(chip, d) * 2 + core
        ours = spectra.at[slot, chip]
        return pltpu.make_async_remote_copy(
            src_ref=ours,
            dst_ref=ours,
            send_sem=block_send.at[slot, d],
            recv_sem=block_recv.at[slot, chip],
            device_id={"rcv": there},
            device_id_type=MESH,
        )

    def arrival(slot, source):
        theirs = spectra.at[slot, source]
        return pltpu.make_async_remote_copy(
            src_ref=theirs,
            dst_ref=theirs,
            send_sem=block_send.at[slot, 0],
            recv_sem=block_recv.at[slot, source],
            device_id={"rcv": me},
            device_id_type=MESH,
        )

    pair = chip // 2

    def convolve(slot, lines, sign, meanwhile=None):
        block = jnp.concatenate(lines, 0).astype(jnp.bfloat16)
        spectra[slot, chip] = block

        def send(d, carry):
            block_copy(slot, d).start()
            return carry

        each_partner(send)
        if meanwhile is not None:
            meanwhile()
        arrival(slot, chip + 1 - 2 * (chip % 2)).wait_recv()

        def multiply(at, totals):
            out = []
            for j in range(freqs):
                left = jnp.concatenate(
                    [spectra[slot, 2 * at + h, deep * j : deep * (j + 1), :] for h in range(2)], 1
                )
                right = matrix[at, j].reshape(2 * LANES, 2 * LANES)
                out.append(
                    totals[j]
                    + lax.dot_general(left, right, NT, preferred_element_type=jnp.float32)
                )
            return tuple(out)

        totals = tuple(jnp.zeros((deep, 2 * LANES), jnp.float32) for _ in range(freqs))
        totals = multiply(pair, totals)

        def step(d, totals):
            at = partner(chip, 2 * d) // 2 if small else (pair + d) % pairs
            arrival(slot, 2 * at).wait_recv()
            arrival(slot, 2 * at + 1).wait_recv()
            return multiply(at, totals)

        if small:
            for d in range(1, pairs):
                totals = step(d, totals)
        else:
            totals = lax.fori_loop(1, pairs, step, totals)

        def sent(d, carry):
            block_copy(slot, d).wait_send()
            return carry

        each_partner(sent)
        result = []
        for t in totals:
            result.append(t[0:half, 0:LANES] - sign * t[half:deep, LANES:])
            result.append(t[half:deep, 0:LANES] + sign * t[0:half, LANES:])
        return result

    def last_copy(u):
        return pltpu.make_async_remote_copy(
            src_ref=leave.at[u],
            dst_ref=arrive.at[u],
            send_sem=last_send.at[u],
            recv_sem=last_recv.at[u],
            device_id={"rcv": twin},
            device_id_type=MESH,
        )

    def hand_over(u, waves):
        turned = [pltpu.roll(wave, LANES - rows, 1) for wave in waves]
        for r in range(phases):
            leave[u, r] = jnp.where(core == 0, turned[r], waves[r])
        last_copy(u).start()
        for r in range(phases):
            out_ref[ours_half, u, r, :] = jnp.where(core == 0, waves[r], turned[r])

    def take_over(u):
        last_copy(u).wait()
        for r in range(phases):
            out_ref[theirs_half, u, r, :] = arrive[u, r]

    lines = first
    for iteration in range(ITERS):
        last = iteration == ITERS - 1
        forward = convolve(0, lines, 1.0, None if iteration else matrix_copy.wait)
        up = to_phases(forward, 3.0 * ticks**-0.5)
        back = to_spectrum([u * n for u, n in zip(up, counts)], ticks**-0.5)
        adjoint = convolve(1, back, -1.0, functools.partial(hand_over, 0, up) if last else None)
        down = to_phases(adjoint, 3.0 * ticks**-0.5)
        if not last:
            change = to_spectrum([u * n for u, n in zip(down, counts)], ticks**-0.5)
            lines = [a + b for a, b in zip(first, change)]
    hand_over(1, down)
    take_over(0)
    take_over(1)


def spread(phases, rows, ticks, count, waves_ref, direct_ref, mute_ref, down_ref, up_ref):
    foci = mute_ref.shape[0]
    base = pl.program_id(0) * count
    comb = combs(4 * phases, phases, ticks)
    ends = mute_ref[...].astype(jnp.float32).astype(jnp.bfloat16)
    lane = lax.broadcasted_iota(jnp.int32, (rows, ticks), 1).astype(jnp.float32)
    which = lax.broadcasted_iota(jnp.int32, (foci, ticks), 0)
    for i in range(count):
        pick = jnp.where(which == base + i, 1.0, 0.0).astype(jnp.bfloat16)
        end = lax.dot_general(ends, pick, TN, preferred_element_type=jnp.float32)
        inside = lane < end
        for u, ref in ((0, up_ref), (1, down_ref)):
            wave = waves_ref[i, u]
            high = wave.astype(jnp.bfloat16).astype(jnp.float32)
            mid = (wave - high).astype(jnp.bfloat16).astype(jnp.float32)
            low = wave - high - mid
            parts = jnp.concatenate([high, mid, low, jnp.zeros_like(low)], 0).astype(jnp.bfloat16)
            field = lax.dot_general(parts, comb, TN, preferred_element_type=jnp.float32)[0:rows]
            field = jnp.where(inside, field, 0.0)
            ref[i] = field if u == 0 else direct_ref[i] + field


def per_device(devices, reflection, direct_wave, mute_start_position):
    freqs = reflection.shape[0]
    foci, rows, ticks = direct_wave.shape
    chips = devices // 2
    phases = 2 * freqs
    half = foci // 2
    vmem = pl.BlockSpec(memory_space=pltpu.VMEM)
    dma = pltpu.SemaphoreType.DMA
    waves = pl.pallas_call(
        functools.partial(iterate, devices, freqs, foci, rows, ticks),
        out_shape=jax.ShapeDtypeStruct((foci, 2, phases, LANES), jnp.float32),
        in_specs=[pl.BlockSpec(memory_space=pl.ANY)] * 3,
        out_specs=vmem,
        scratch_shapes=[
            pltpu.VMEM(reflection.shape, jnp.bfloat16),
            pltpu.VMEM(direct_wave.shape, jnp.float32),
            pltpu.VMEM(mute_start_position.shape, jnp.int32),
            pltpu.VMEM((chips // 2, freqs, 2, LANES, 2 * LANES), jnp.bfloat16),
            pltpu.VMEM((2, chips, 2 * freqs * half, LANES), jnp.bfloat16),
            pltpu.VMEM((phases + 1, foci, LANES), jnp.float32),
            pltpu.VMEM((phases + 1, half, LANES), jnp.float32),
            pltpu.VMEM((2, phases, half, LANES), jnp.float32),
            pltpu.VMEM((2, phases, half, LANES), jnp.float32),
            dma((4,)), dma, dma, dma, dma,
            dma((2, chips)), dma((2, chips)),
            dma((2,)), dma((2,)),
        ],
        compiler_params=pltpu.CompilerParams(
            collective_id=0, has_side_effects=True, vmem_limit_bytes=60 * 2**20
        ),
    )(reflection, direct_wave, mute_start_position)
    count = 8
    return tuple(
        pl.pallas_call(
            functools.partial(spread, phases, rows, ticks, count),
            grid=(foci // count,),
            out_shape=[jax.ShapeDtypeStruct(direct_wave.shape, jnp.float32)] * 2,
            in_specs=[
                pl.BlockSpec((count, 2, phases, LANES), lambda i: (i, 0, 0, 0)),
                pl.BlockSpec((count, rows, ticks), lambda i: (i, 0, 0)),
                pl.BlockSpec((foci, rows), lambda i: (0, 0)),
            ],
            out_specs=[pl.BlockSpec((count, rows, ticks), lambda i: (i, 0, 0))] * 2,
            compiler_params=pltpu.CompilerParams(vmem_limit_bytes=16 * 2**20),
        )(waves, direct_wave, mute_start_position)
    )


def solution(mesh):
    placed = (P("grp", None, "rcv", None), P("grp", "rcv", None), P("grp", "rcv"))
    return jax.shard_map(
        functools.partial(per_device, mesh.shape["rcv"]),
        mesh=mesh,
        in_specs=placed,
        out_specs=(P("grp", "rcv", None), P("grp", "rcv", None)),
        check_vma=False,
    )
```

```python
import functools
import math

import jax
import jax.numpy as jnp
from jax import lax
from jax.experimental import pallas as pl
from jax.experimental.pallas import tpu as pltpu
from jax.sharding import PartitionSpec as P

ITERS = 4
LANES = 128
NT = (((1,), (1,)), ((), ()))
TN = (((0,), (0,)), ((), ()))
MESH = pl.DeviceIdType.MESH


def tables(freqs):
    phases = 2 * freqs
    period = 2 * phases
    angle = [
        [2.0 * math.pi * ((r * (2 * j + 1)) % period) / period for j in range(freqs)]
        for r in range(phases)
    ]
    cosine = [[math.cos(a) for a in row] for row in angle]
    sine = [[math.sin(a) for a in row] for row in angle]
    return cosine, sine


def combs(rows, phases, ticks):
    row = lax.broadcasted_iota(jnp.int32, (rows, ticks), 0) % phases
    tick = lax.broadcasted_iota(jnp.int32, (rows, ticks), 1)
    sign = (1 - 2 * ((tick // phases) % 2)).astype(jnp.float32)
    return jnp.where(tick % phases == row, sign, 0.0).astype(jnp.bfloat16)


def add_up(terms):
    terms = list(terms)
    while len(terms) > 1:
        pairs = [a + b for a, b in zip(terms[::2], terms[1::2])]
        terms = pairs + ([terms[-1]] if len(terms) % 2 else [])
    return terms[0]


def iterate(
    devices, freqs, foci, rows, ticks,
    refl_hbm, direct_hbm, mute_hbm, out_ref,
    refl_ref, direct_ref, mute_ref, matrix, spectra, own, other, leave, arrive,
    fetched, matrix_send, matrix_recv, own_send, own_recv,
    block_send, block_recv, last_send, last_recv,
):
    chips = devices // 2
    pairs = chips // 2
    phases = 2 * freqs
    half = foci // 2
    width = 2 * rows
    deep = 2 * half
    me = lax.axis_index("rcv")
    core = me % 2
    chip = me // 2
    twin = chip * 2 + (1 - core)
    cosine, sine = tables(freqs)

    theirs_half = pl.ds((1 - core) * half, half)
    ours_half = pl.ds(core * half, half)
    fetches = [
        pltpu.make_async_copy(direct_hbm.at[theirs_half], direct_ref.at[theirs_half], fetched.at[0]),
        pltpu.make_async_copy(mute_hbm, mute_ref, fetched.at[1]),
        pltpu.make_async_copy(direct_hbm.at[ours_half], direct_ref.at[ours_half], fetched.at[2]),
        pltpu.make_async_copy(refl_hbm, refl_ref, fetched.at[3]),
    ]
    for fetch in fetches:
        fetch.start()

    barrier = pltpu.get_barrier_semaphore()
    pl.semaphore_signal(barrier, inc=1, device_id={"rcv": twin}, device_id_type=MESH)

    def greet(d, carry):
        there = ((chip + d) % chips) * 2 + core
        pl.semaphore_signal(barrier, inc=1, device_id={"rcv": there}, device_id_type=MESH)
        return carry

    lax.fori_loop(1, chips, greet, 0)

    own[...] = jnp.zeros_like(own)
    comb = combs(2 * phases, phases, ticks)

    def sum_phases(start):
        for i in range(half):
            p = start + i
            wave = direct_ref[p]
            high = wave.astype(jnp.bfloat16)
            low = (wave - high.astype(jnp.float32)).astype(jnp.bfloat16)
            sums = lax.dot_general(comb, high, NT, preferred_element_type=jnp.float32)
            sums += lax.dot_general(comb, low, NT, preferred_element_type=jnp.float32)
            own[0:phases, p, 0:rows] = sums[0:phases]

    fetches[0].wait()
    sum_phases((1 - core) * half)
    fetches[1].wait()
    own[phases, :, 0:rows] = mute_ref[...].astype(jnp.float32)

    pl.semaphore_wait(barrier, chips)

    own_copy = pltpu.make_async_remote_copy(
        src_ref=own.at[:, pl.ds(pl.multiple_of((1 - core) * half, 8), half), :],
        dst_ref=other,
        send_sem=own_send,
        recv_sem=own_recv,
        device_id={"rcv": twin},
        device_id_type=MESH,
    )
    own_copy.start()
    fetches[2].wait()
    sum_phases(core * half)
    fetches[3].wait()

    place = pl.ds(pl.multiple_of(core * rows, 16), rows)
    rest = LANES - width
    for j in range(freqs):
        for c in range(2):
            if rest:
                matrix[:, j, c, width:LANES, :] = jnp.zeros((pairs, rest, 2 * LANES), jnp.bfloat16)
            for k in range(chips):
                part = refl_ref[j, c, :, k * width : (k + 1) * width]
                if rest:
                    part = jnp.concatenate([part, jnp.zeros((rows, rest), jnp.bfloat16)], 1)
                matrix[k // 2, j, c, place, (k % 2) * LANES : (k % 2 + 1) * LANES] = part
    matrix_copy = pltpu.make_async_remote_copy(
        src_ref=matrix.at[:, :, :, place, :],
        dst_ref=matrix.at[:, :, :, place, :],
        send_sem=matrix_send,
        recv_sem=matrix_recv,
        device_id={"rcv": twin},
        device_id_type=MESH,
    )
    matrix_copy.start()

    own_copy.wait()

    def whole(a, b):
        left = jnp.where(core == 0, a, b)
        right = jnp.where(core == 0, b, a)
        return left + pltpu.roll(right, rows, 1)

    mine = pl.ds(pl.multiple_of(core * half, 8), half)
    sums = [whole(own[r, mine, :], other[r]) for r in range(phases + 1)]
    ends = sums.pop()
    counts = [jnp.floor((ends + (phases - 1 - r)) * (1.0 / phases)) for r in range(phases)]

    def to_spectrum(values, scale):
        lines = []
        for j in range(freqs):
            lines.append(add_up(values[r] * (scale * cosine[r][j]) for r in range(phases)))
            lines.append(add_up(values[r] * (-scale * sine[r][j]) for r in range(phases)))
        return lines

    def to_phases(lines, scale):
        return [
            add_up(
                lines[2 * j + c] * (scale * (cosine[r][j], -sine[r][j])[c])
                for j in range(freqs)
                for c in range(2)
            )
            for r in range(phases)
        ]

    first = to_spectrum(sums, ticks**-0.5)

    small = chips == 8

    def line(d):
        upper = (chip // 2) // 2
        lower = (chip // 2) % 2
        return (chip // 2, 2 * upper + 1 - lower, 2 - upper, 3 * (1 - upper))[d]

    def partner(number, d):
        if not small:
            return (number + d) % chips
        side = chip % 2
        return 2 * line(d // 2) + (1 - side if d % 2 else side)

    def each_partner(body):
        if small:
            for d in range(chips - 1, 0, -1):
                body(d, 0)
        else:
            lax.fori_loop(1, chips, body, 0)

    def block_copy(slot, d):
        there = partner(chip, d) * 2 + core
        ours = spectra.at[slot, chip]
        return pltpu.make_async_remote_copy(
            src_ref=ours,
            dst_ref=ours,
            send_sem=block_send.at[slot, d],
            recv_sem=block_recv.at[slot, chip],
            device_id={"rcv": there},
            device_id_type=MESH,
        )

    def arrival(slot, source):
        theirs = spectra.at[slot, source]
        return pltpu.make_async_remote_copy(
            src_ref=theirs,
            dst_ref=theirs,
            send_sem=block_send.at[slot, 0],
            recv_sem=block_recv.at[slot, source],
            device_id={"rcv": me},
            device_id_type=MESH,
        )

    pair = chip // 2
    packed = spectra.shape[2] < freqs * deep

    def convolve(slot, lines, sign, meanwhile=None):
        tiles = [jnp.concatenate(lines[2 * j : 2 * j + 2], 0) for j in range(freqs)]
        if packed:
            spare = tiles.pop()
            lane = lax.broadcasted_iota(jnp.int32, spare.shape, 1)
            tiles = [
                jnp.where(lane < width, tile, pltpu.roll(spare, width - rest * i, 1))
                for i, tile in enumerate(tiles)
            ]
        spectra[slot, chip] = jnp.concatenate(tiles, 0).astype(jnp.bfloat16)

        def send(d, carry):
            block_copy(slot, d).start()
            return carry

        def sent(d, carry):
            block_copy(slot, d).wait_send()
            return carry

        each_partner(send)
        if meanwhile is not None:
            meanwhile()
        arrival(slot, chip + 1 - 2 * (chip % 2)).wait_recv()

        def unpack(source):
            held = spectra.shape[2] // deep
            tiles = [spectra[slot, source, deep * j : deep * (j + 1), :] for j in range(held)]
            if packed:
                lane = lax.broadcasted_iota(jnp.int32, (deep, LANES), 1)
                spare = None
                for i in range(held - 1, -1, -1):
                    piece = pltpu.roll(tiles[i].astype(jnp.float32), LANES - width + rest * i, 1)
                    spare = piece if spare is None else jnp.where(lane < rest * (i + 1), piece, spare)
                tiles.append(spare.astype(jnp.bfloat16))
            return tiles

        def multiply(at, totals):
            out = []
            sides = [unpack(2 * at), unpack(2 * at + 1)]
            for j in range(freqs):
                left = jnp.concatenate([side[j] for side in sides], 1)
                right = matrix[at, j].reshape(2 * LANES, 2 * LANES)
                out.append(
                    totals[j]
                    + lax.dot_general(left, right, NT, preferred_element_type=jnp.float32)
                )
            return tuple(out)

        totals = tuple(jnp.zeros((deep, 2 * LANES), jnp.float32) for _ in range(freqs))
        totals = multiply(pair, totals)

        def step(d, totals):
            at = line(d) if small else (pair + d) % pairs
            arrival(slot, 2 * at).wait_recv()
            arrival(slot, 2 * at + 1).wait_recv()
            return multiply(at, totals)

        if small:
            for d in range(1, pairs):
                if d == pairs - 1:
                    each_partner(sent)
                totals = step(d, totals)
        else:
            totals = lax.fori_loop(1, pairs, step, totals)
            each_partner(sent)

        result = []
        for t in totals:
            result.append(t[0:half, 0:LANES] - sign * t[half:deep, LANES:])
            result.append(t[half:deep, 0:LANES] + sign * t[0:half, LANES:])
        return result

    def last_copy(u):
        return pltpu.make_async_remote_copy(
            src_ref=leave.at[u],
            dst_ref=arrive.at[u],
            send_sem=last_send.at[u],
            recv_sem=last_recv.at[u],
            device_id={"rcv": twin},
            device_id_type=MESH,
        )

    def hand_over(u, waves):
        turned = [pltpu.roll(wave, LANES - rows, 1) for wave in waves]
        for r in range(phases):
            leave[u, r] = jnp.where(core == 0, turned[r], waves[r])
        last_copy(u).start()
        for r in range(phases):
            out_ref[ours_half, u, r, :] = jnp.where(core == 0, waves[r], turned[r])

    def take_over(u):
        last_copy(u).wait()
        for r in range(phases):
            out_ref[theirs_half, u, r, :] = arrive[u, r]

    lines = first
    for iteration in range(ITERS):
        last = iteration == ITERS - 1
        forward = convolve(0, lines, 1.0, None if iteration else matrix_copy.wait)
        up = to_phases(forward, 3.0 * ticks**-0.5)
        back = to_spectrum([u * n for u, n in zip(up, counts)], ticks**-0.5)
        adjoint = convolve(1, back, -1.0, functools.partial(hand_over, 0, up) if last else None)
        down = to_phases(adjoint, 3.0 * ticks**-0.5)
        if not last:
            change = to_spectrum([u * n for u, n in zip(down, counts)], ticks**-0.5)
            lines = [a + b for a, b in zip(first, change)]
    hand_over(1, down)
    take_over(0)
    take_over(1)


def spread(phases, rows, ticks, count, waves_ref, direct_ref, mute_ref, down_ref, up_ref):
    foci = mute_ref.shape[0]
    base = pl.program_id(0) * count
    comb = combs(4 * phases, phases, ticks)
    ends = mute_ref[...].astype(jnp.float32).astype(jnp.bfloat16)
    lane = lax.broadcasted_iota(jnp.int32, (rows, ticks), 1).astype(jnp.float32)
    which = lax.broadcasted_iota(jnp.int32, (foci, ticks), 0)
    for i in range(count):
        pick = jnp.where(which == base + i, 1.0, 0.0).astype(jnp.bfloat16)
        end = lax.dot_general(ends, pick, TN, preferred_element_type=jnp.float32)
        inside = lane < end
        for u, ref in ((0, up_ref), (1, down_ref)):
            wave = waves_ref[i, u]
            high = wave.astype(jnp.bfloat16).astype(jnp.float32)
            mid = (wave - high).astype(jnp.bfloat16).astype(jnp.float32)
            low = wave - high - mid
            parts = jnp.concatenate([high, mid, low, jnp.zeros_like(low)], 0).astype(jnp.bfloat16)
            field = lax.dot_general(parts, comb, TN, preferred_element_type=jnp.float32)[0:rows]
            field = jnp.where(inside, field, 0.0)
            ref[i] = field if u == 0 else direct_ref[i] + field


def per_device(devices, reflection, direct_wave, mute_start_position):
    freqs = reflection.shape[0]
    foci, rows, ticks = direct_wave.shape
    chips = devices // 2
    phases = 2 * freqs
    half = foci // 2
    rest = LANES - 2 * rows
    packed = int(rest > 0 and rest * (freqs - 1) == 2 * rows)
    vmem = pl.BlockSpec(memory_space=pltpu.VMEM)
    dma = pltpu.SemaphoreType.DMA
    waves = pl.pallas_call(
        functools.partial(iterate, devices, freqs, foci, rows, ticks),
        out_shape=jax.ShapeDtypeStruct((foci, 2, phases, LANES), jnp.float32),
        in_specs=[pl.BlockSpec(memory_space=pl.ANY)] * 3,
        out_specs=vmem,
        scratch_shapes=[
            pltpu.VMEM(reflection.shape, jnp.bfloat16),
            pltpu.VMEM(direct_wave.shape, jnp.float32),
            pltpu.VMEM(mute_start_position.shape, jnp.int32),
            pltpu.VMEM((chips // 2, freqs, 2, LANES, 2 * LANES), jnp.bfloat16),
            pltpu.VMEM((2, chips, 2 * half * (freqs - packed), LANES), jnp.bfloat16),
            pltpu.VMEM((phases + 1, foci, LANES), jnp.float32),
            pltpu.VMEM((phases + 1, half, LANES), jnp.float32),
            pltpu.VMEM((2, phases, half, LANES), jnp.float32),
            pltpu.VMEM((2, phases, half, LANES), jnp.float32),
            dma((4,)), dma, dma, dma, dma,
            dma((2, chips)), dma((2, chips)),
            dma((2,)), dma((2,)),
        ],
        compiler_params=pltpu.CompilerParams(
            collective_id=0, has_side_effects=True, vmem_limit_bytes=60 * 2**20
        ),
    )(reflection, direct_wave, mute_start_position)
    count = 8
    return tuple(
        pl.pallas_call(
            functools.partial(spread, phases, rows, ticks, count),
            grid=(foci // count,),
            out_shape=[jax.ShapeDtypeStruct(direct_wave.shape, jnp.float32)] * 2,
            in_specs=[
                pl.BlockSpec((count, 2, phases, LANES), lambda i: (i, 0, 0, 0)),
                pl.BlockSpec((count, rows, ticks), lambda i: (i, 0, 0)),
                pl.BlockSpec((foci, rows), lambda i: (0, 0)),
            ],
            out_specs=[pl.BlockSpec((count, rows, ticks), lambda i: (i, 0, 0))] * 2,
            compiler_params=pltpu.CompilerParams(vmem_limit_bytes=16 * 2**20),
        )(waves, direct_wave, mute_start_position)
    )


def solution(mesh):
    placed = (P("grp", None, "rcv", None), P("grp", "rcv", None), P("grp", "rcv"))
    return jax.shard_map(
        functools.partial(per_device, mesh.shape["rcv"]),
        mesh=mesh,
        in_specs=placed,
        out_specs=(P("grp", "rcv", None), P("grp", "rcv", None)),
        check_vma=False,
    )
```

```python
import functools
import math

import jax
import jax.numpy as jnp
from jax import lax
from jax.experimental import pallas as pl
from jax.experimental.pallas import tpu as pltpu
from jax.sharding import PartitionSpec as P

ITERS = 4
LANES = 128
NT = (((1,), (1,)), ((), ()))
TN = (((0,), (0,)), ((), ()))
MESH = pl.DeviceIdType.MESH


def tables(freqs):
    phases = 2 * freqs
    period = 2 * phases
    angle = [
        [2.0 * math.pi * ((r * (2 * j + 1)) % period) / period for j in range(freqs)]
        for r in range(phases)
    ]
    cosine = [[math.cos(a) for a in row] for row in angle]
    sine = [[math.sin(a) for a in row] for row in angle]
    return cosine, sine


def combs(rows, phases, ticks):
    row = lax.broadcasted_iota(jnp.int32, (rows, ticks), 0) % phases
    tick = lax.broadcasted_iota(jnp.int32, (rows, ticks), 1)
    sign = (1 - 2 * ((tick // phases) % 2)).astype(jnp.float32)
    return jnp.where(tick % phases == row, sign, 0.0).astype(jnp.bfloat16)


def add_up(terms):
    terms = list(terms)
    while len(terms) > 1:
        pairs = [a + b for a, b in zip(terms[::2], terms[1::2])]
        terms = pairs + ([terms[-1]] if len(terms) % 2 else [])
    return terms[0]


def iterate(
    devices, freqs, foci, rows, ticks,
    refl_hbm, direct_hbm, mute_hbm, out_ref,
    refl_ref, direct_ref, mute_ref, matrix, spectra, own, other, leave, arrive,
    fetched, matrix_send, matrix_recv, own_send, own_recv,
    block_send, block_recv, last_send, last_recv,
):
    chips = devices // 2
    pairs = chips // 2
    phases = 2 * freqs
    half = foci // 2
    width = 2 * rows
    deep = 2 * half
    rest = LANES - width
    me = lax.axis_index("rcv")
    core = me % 2
    chip = me // 2
    twin = chip * 2 + (1 - core)
    cosine, sine = tables(freqs)

    theirs_half = pl.ds((1 - core) * half, half)
    ours_half = pl.ds(core * half, half)
    fetches = [
        pltpu.make_async_copy(direct_hbm.at[theirs_half], direct_ref.at[theirs_half], fetched.at[0]),
        pltpu.make_async_copy(mute_hbm, mute_ref, fetched.at[1]),
        pltpu.make_async_copy(direct_hbm.at[ours_half], direct_ref.at[ours_half], fetched.at[2]),
        pltpu.make_async_copy(refl_hbm, refl_ref, fetched.at[3]),
    ]
    for fetch in fetches:
        fetch.start()

    barrier = pltpu.get_barrier_semaphore()
    pl.semaphore_signal(barrier, inc=1, device_id={"rcv": twin}, device_id_type=MESH)

    def greet(d, carry):
        there = ((chip + d) % chips) * 2 + core
        pl.semaphore_signal(barrier, inc=1, device_id={"rcv": there}, device_id_type=MESH)
        return carry

    lax.fori_loop(1, chips, greet, 0)

    own[...] = jnp.zeros_like(own)
    comb = combs(2 * phases, phases, ticks)

    def sum_phases(start):
        for i in range(half):
            p = start + i
            wave = direct_ref[p]
            high = wave.astype(jnp.bfloat16)
            low = (wave - high.astype(jnp.float32)).astype(jnp.bfloat16)
            sums = lax.dot_general(comb, high, NT, preferred_element_type=jnp.float32)
            sums += lax.dot_general(comb, low, NT, preferred_element_type=jnp.float32)
            own[0:phases, p, 0:rows] = sums[0:phases]

    fetches[0].wait()
    sum_phases((1 - core) * half)
    fetches[1].wait()
    own[phases, :, 0:rows] = mute_ref[...].astype(jnp.float32)

    pl.semaphore_wait(barrier, chips)

    own_copy = pltpu.make_async_remote_copy(
        src_ref=own.at[:, pl.ds(pl.multiple_of((1 - core) * half, 8), half), :],
        dst_ref=other,
        send_sem=own_send,
        recv_sem=own_recv,
        device_id={"rcv": twin},
        device_id_type=MESH,
    )
    own_copy.start()
    fetches[2].wait()
    sum_phases(core * half)


    def lay_out():
        fetches[3].wait()
        place = pl.ds(pl.multiple_of(core * rows, 16), rows)
        for j in range(freqs):
            for c in range(2):
                if rest:
                    matrix[:, j, c, width:LANES, :] = jnp.zeros((pairs, rest, 2 * LANES), jnp.bfloat16)
                for k in range(chips):
                    part = refl_ref[j, c, :, k * width : (k + 1) * width]
                    if rest:
                        part = jnp.concatenate([part, jnp.zeros((rows, rest), jnp.bfloat16)], 1)
                    matrix[k // 2, j, c, place, (k % 2) * LANES : (k % 2 + 1) * LANES] = part
        matrix_copy = pltpu.make_async_remote_copy(
            src_ref=matrix.at[:, :, :, place, :],
            dst_ref=matrix.at[:, :, :, place, :],
            send_sem=matrix_send,
            recv_sem=matrix_recv,
            device_id={"rcv": twin},
            device_id_type=MESH,
        )
        matrix_copy.start()
        matrix_copy.wait()

    own_copy.wait()

    def whole(a, b):
        left = jnp.where(core == 0, a, b)
        right = jnp.where(core == 0, b, a)
        return left + pltpu.roll(right, rows, 1)

    mine = pl.ds(pl.multiple_of(core * half, 8), half)
    sums = [whole(own[r, mine, :], other[r]) for r in range(phases + 1)]
    ends = sums.pop()
    counts = [jnp.floor((ends + (phases - 1 - r)) * (1.0 / phases)) for r in range(phases)]

    def to_spectrum(values, scale):
        lines = []
        for j in range(freqs):
            lines.append(add_up(values[r] * (scale * cosine[r][j]) for r in range(phases)))
            lines.append(add_up(values[r] * (-scale * sine[r][j]) for r in range(phases)))
        return lines

    def to_phases(lines, scale):
        return [
            add_up(
                lines[2 * j + c] * (scale * (cosine[r][j], -sine[r][j])[c])
                for j in range(freqs)
                for c in range(2)
            )
            for r in range(phases)
        ]

    first = to_spectrum(sums, ticks**-0.5)

    small = chips == 8

    def line(d):
        upper = (chip // 2) // 2
        lower = (chip // 2) % 2
        return (chip // 2, 2 * upper + 1 - lower, 2 - upper, 3 * (1 - upper))[d]

    def partner(number, d):
        if not small:
            return (number + d) % chips
        side = chip % 2
        return 2 * line(d // 2) + (1 - side if d % 2 else side)

    def each_partner(body):
        if small:
            for d in range(chips - 1, 0, -1):
                body(d, 0)
        else:
            lax.fori_loop(1, chips, body, 0)

    def block_copy(slot, d):
        there = partner(chip, d) * 2 + core
        ours = spectra.at[slot, chip]
        return pltpu.make_async_remote_copy(
            src_ref=ours,
            dst_ref=ours,
            send_sem=block_send.at[slot, d],
            recv_sem=block_recv.at[slot, chip],
            device_id={"rcv": there},
            device_id_type=MESH,
        )

    def arrival(slot, source):
        theirs = spectra.at[slot, source]
        return pltpu.make_async_remote_copy(
            src_ref=theirs,
            dst_ref=theirs,
            send_sem=block_send.at[slot, 0],
            recv_sem=block_recv.at[slot, source],
            device_id={"rcv": me},
            device_id_type=MESH,
        )

    pair = chip // 2
    packed = spectra.shape[2] < freqs * deep

    def convolve(slot, lines, sign, meanwhile=None):
        tiles = [jnp.concatenate(lines[2 * j : 2 * j + 2], 0) for j in range(freqs)]
        if packed:
            spare = tiles.pop()
            lane = lax.broadcasted_iota(jnp.int32, spare.shape, 1)
            tiles = [
                jnp.where(lane < width, tile, pltpu.roll(spare, width - rest * i, 1))
                for i, tile in enumerate(tiles)
            ]
        spectra[slot, chip] = jnp.concatenate(tiles, 0).astype(jnp.bfloat16)

        def send(d, carry):
            block_copy(slot, d).start()
            return carry

        def sent(d, carry):
            block_copy(slot, d).wait_send()
            return carry

        each_partner(send)
        if meanwhile is not None:
            meanwhile()
        arrival(slot, chip + 1 - 2 * (chip % 2)).wait_recv()

        def unpack(source):
            held = spectra.shape[2] // deep
            tiles = [spectra[slot, source, deep * j : deep * (j + 1), :] for j in range(held)]
            if packed:
                lane = lax.broadcasted_iota(jnp.int32, (deep, LANES), 1)
                spare = None
                for i in range(held - 1, -1, -1):
                    piece = pltpu.roll(tiles[i].astype(jnp.float32), LANES - width + rest * i, 1)
                    spare = piece if spare is None else jnp.where(lane < rest * (i + 1), piece, spare)
                tiles.append(spare.astype(jnp.bfloat16))
            return tiles

        def multiply(at, totals):
            out = []
            sides = [unpack(2 * at), unpack(2 * at + 1)]
            for j in range(freqs):
                left = jnp.concatenate([side[j] for side in sides], 1)
                right = matrix[at, j].reshape(2 * LANES, 2 * LANES)
                out.append(
                    totals[j]
                    + lax.dot_general(left, right, NT, preferred_element_type=jnp.float32)
                )
            return tuple(out)

        totals = tuple(jnp.zeros((deep, 2 * LANES), jnp.float32) for _ in range(freqs))
        totals = multiply(pair, totals)

        def step(d, totals):
            at = line(d) if small else (pair + d) % pairs
            arrival(slot, 2 * at).wait_recv()
            arrival(slot, 2 * at + 1).wait_recv()
            return multiply(at, totals)

        if small:
            for d in range(1, pairs):
                if d == pairs - 1:
                    each_partner(sent)
                totals = step(d, totals)
        else:
            totals = lax.fori_loop(1, pairs, step, totals)
            each_partner(sent)

        result = []
        for t in totals:
            result.append(t[0:half, 0:LANES] - sign * t[half:deep, LANES:])
            result.append(t[half:deep, 0:LANES] + sign * t[0:half, LANES:])
        return result

    def last_copy(u):
        return pltpu.make_async_remote_copy(
            src_ref=leave.at[u],
            dst_ref=arrive.at[u],
            send_sem=last_send.at[u],
            recv_sem=last_recv.at[u],
            device_id={"rcv": twin},
            device_id_type=MESH,
        )

    def hand_over(u, waves):
        turned = [pltpu.roll(wave, LANES - rows, 1) for wave in waves]
        for r in range(phases):
            leave[u, r] = jnp.where(core == 0, turned[r], waves[r])
        last_copy(u).start()
        for r in range(phases):
            out_ref[ours_half, u, r, :] = jnp.where(core == 0, waves[r], turned[r])

    def take_over(u):
        last_copy(u).wait()
        for r in range(phases):
            out_ref[theirs_half, u, r, :] = arrive[u, r]

    lines = first
    for iteration in range(ITERS):
        last = iteration == ITERS - 1
        forward = convolve(0, lines, 1.0, None if iteration else lay_out)
        up = to_phases(forward, 3.0 * ticks**-0.5)
        back = to_spectrum([u * n for u, n in zip(up, counts)], ticks**-0.5)
        adjoint = convolve(1, back, -1.0, functools.partial(hand_over, 0, up) if last else None)
        down = to_phases(adjoint, 3.0 * ticks**-0.5)
        if not last:
            change = to_spectrum([u * n for u, n in zip(down, counts)], ticks**-0.5)
            lines = [a + b for a, b in zip(first, change)]
    hand_over(1, down)
    take_over(0)
    take_over(1)


def spread(phases, rows, ticks, count, waves_ref, direct_ref, mute_ref, down_ref, up_ref):
    foci = mute_ref.shape[0]
    base = pl.program_id(0) * count
    comb = combs(4 * phases, phases, ticks)
    ends = mute_ref[...].astype(jnp.float32).astype(jnp.bfloat16)
    lane = lax.broadcasted_iota(jnp.int32, (rows, ticks), 1).astype(jnp.float32)
    which = lax.broadcasted_iota(jnp.int32, (foci, ticks), 0)
    for i in range(count):
        pick = jnp.where(which == base + i, 1.0, 0.0).astype(jnp.bfloat16)
        end = lax.dot_general(ends, pick, TN, preferred_element_type=jnp.float32)
        inside = lane < end
        for u, ref in ((0, up_ref), (1, down_ref)):
            wave = waves_ref[i, u]
            high = wave.astype(jnp.bfloat16).astype(jnp.float32)
            mid = (wave - high).astype(jnp.bfloat16).astype(jnp.float32)
            low = wave - high - mid
            parts = jnp.concatenate([high, mid, low, jnp.zeros_like(low)], 0).astype(jnp.bfloat16)
            field = lax.dot_general(parts, comb, TN, preferred_element_type=jnp.float32)[0:rows]
            field = jnp.where(inside, field, 0.0)
            ref[i] = field if u == 0 else direct_ref[i] + field


def per_device(devices, reflection, direct_wave, mute_start_position):
    freqs = reflection.shape[0]
    foci, rows, ticks = direct_wave.shape
    chips = devices // 2
    phases = 2 * freqs
    half = foci // 2
    rest = LANES - 2 * rows
    packed = int(rest > 0 and rest * (freqs - 1) == 2 * rows)
    vmem = pl.BlockSpec(memory_space=pltpu.VMEM)
    dma = pltpu.SemaphoreType.DMA
    waves = pl.pallas_call(
        functools.partial(iterate, devices, freqs, foci, rows, ticks),
        out_shape=jax.ShapeDtypeStruct((foci, 2, phases, LANES), jnp.float32),
        in_specs=[pl.BlockSpec(memory_space=pl.ANY)] * 3,
        out_specs=vmem,
        scratch_shapes=[
            pltpu.VMEM(reflection.shape, jnp.bfloat16),
            pltpu.VMEM(direct_wave.shape, jnp.float32),
            pltpu.VMEM(mute_start_position.shape, jnp.int32),
            pltpu.VMEM((chips // 2, freqs, 2, LANES, 2 * LANES), jnp.bfloat16),
            pltpu.VMEM((2, chips, 2 * half * (freqs - packed), LANES), jnp.bfloat16),
            pltpu.VMEM((phases + 1, foci, LANES), jnp.float32),
            pltpu.VMEM((phases + 1, half, LANES), jnp.float32),
            pltpu.VMEM((2, phases, half, LANES), jnp.float32),
            pltpu.VMEM((2, phases, half, LANES), jnp.float32),
            dma((4,)), dma, dma, dma, dma,
            dma((2, chips)), dma((2, chips)),
            dma((2,)), dma((2,)),
        ],
        compiler_params=pltpu.CompilerParams(
            collective_id=0, has_side_effects=True, vmem_limit_bytes=60 * 2**20
        ),
    )(reflection, direct_wave, mute_start_position)
    count = 8
    return tuple(
        pl.pallas_call(
            functools.partial(spread, phases, rows, ticks, count),
            grid=(foci // count,),
            out_shape=[jax.ShapeDtypeStruct(direct_wave.shape, jnp.float32)] * 2,
            in_specs=[
                pl.BlockSpec((count, 2, phases, LANES), lambda i: (i, 0, 0, 0)),
                pl.BlockSpec((count, rows, ticks), lambda i: (i, 0, 0)),
                pl.BlockSpec((foci, rows), lambda i: (0, 0)),
            ],
            out_specs=[pl.BlockSpec((count, rows, ticks), lambda i: (i, 0, 0))] * 2,
            compiler_params=pltpu.CompilerParams(vmem_limit_bytes=16 * 2**20),
        )(waves, direct_wave, mute_start_position)
    )


def solution(mesh):
    placed = (P("grp", None, "rcv", None), P("grp", "rcv", None), P("grp", "rcv"))
    return jax.shard_map(
        functools.partial(per_device, mesh.shape["rcv"]),
        mesh=mesh,
        in_specs=placed,
        out_specs=(P("grp", "rcv", None), P("grp", "rcv", None)),
        check_vma=False,
    )
```
